1024 devices in a mesh: dp: 16 (over z_hi, y), expert: 16 (over z_lo, core), tp: 4 (over x).
Axes of the slice: x: 4, y: 4, z: 32 (z_hi: 4, z_lo: 8; z = z_hi * 8 + z_lo), core: 2. Of those that a mesh axis runs over, the one named last changes fastest.
Arguments:
- tokens: bfloat16 [2048, 3584], P(('dp', 'expert'), 'tp'), may hold values from -6 to 6
- out_grad: bfloat16 [2048, 3584], P(('dp', 'expert'), 'tp'), may hold values from -6 to 6
- expert_ids: int32 [2048, 2], P(('dp', 'expert')), may hold values from 0 to 15, all different within a row; in each aligned block of 8 rows (0 to 7, 8 to 15, ...) at most 2 rows name the same one
- gate_probs: float32 [2048, 2], P(('dp', 'expert')), may hold values from 0.1 to 1
- w_gate: bfloat16 [16, 3584, 4864], P('expert', 'tp', 'dp'), may hold values from -0.09375 to 0.09375
- w_up: bfloat16 [16, 3584, 4864], P('expert', 'tp', 'dp'), may hold values from -0.09375 to 0.09375
- w_down: bfloat16 [16, 4864, 3584], P('expert', 'dp', 'tp'), may hold values from -0.078125 to 0.078125
Outputs:
- mixed: bfloat16 [2048, 3584], P(('dp', 'expert'), 'tp')
- grad_tokens: bfloat16 [2048, 3584], P(('dp', 'expert'), 'tp')
- grad_gate: bfloat16 [16, 3584, 4864], P('expert', 'tp', 'dp')
- grad_up: bfloat16 [16, 3584, 4864], P('expert', 'tp', 'dp')
- grad_down: bfloat16 [16, 4864, 3584], P('expert', 'dp', 'tp')
The draws below stay inside these ranges and needn't reach their ends.
Inputs may be any that keep to these rules, and one draw needn't show every extreme that they name: `expert_ids`: the two ids of a token differ. In each aligned block of 8 tokens (the tokens of one device) no expert is named by more than 2 tokens, a bound that some block reaches.
All inputs are finite; a program needn't handle non-finite values.
Results may differ from the reference program's by a relative error of at most 0.0065.
Values may be sent and summed in bfloat16 or wider, within the bound.
A program may use at most 32 MiB of HBM per device.

```python
import math
import jax
import jax.numpy as jnp
import numpy as np
from jax import lax

D = 3584
HE = 4864
TOK_DEV = 8
EXPERTS = 16
CAP = 2
TOKENS = 2048
N_DP = 16
N_EXPERT = 16


def shard_levels(key, shape, cuts, least, largest):
    gain = 1.0
    for axis_at, parts in cuts:
        steps = jax.random.uniform(jax.random.fold_in(jax.random.fold_in(key, 6), axis_at), (parts,), jnp.float32, least / len(cuts), largest / len(cuts))
        gain = gain * jnp.repeat(jnp.exp(steps), shape[axis_at] // parts).reshape((-1,) + (1,) * (len(shape) - 1 - axis_at))
    return gain


def shared_out(own_key, own, number, rows, count, top, most, skew):
    order = jax.random.permutation(own_key, count)
    heavy_load, ordinary = shares(count, rows * top, most, skew, True), shares(count, rows * top, most, skew, False)
    places = jnp.arange(count)

    def named(tallies, offset_by):
        used = int((tallies > 0).sum())
        fixed = max(1, used // 4)
        shifted = fixed + (places - fixed + offset_by * (used - fixed)) % max(1, count - fixed)
        return jnp.zeros((count,), jnp.int32).at[order[jnp.where(places < fixed, places, shifted)]].set(jnp.asarray(tallies, jnp.int32))

    tallies = jnp.where(number % 4 == 0, named(heavy_load, number // 4), named(ordinary, number - number // 4 - 1))
    mixed = jax.random.permutation(jax.random.fold_in(own, 3), count)
    donor, sink = mixed[0:count // 2 * 2:2], mixed[1:count // 2 * 2:2]
    slack = jnp.minimum(tallies[donor] - 1, most - tallies[sink]) // 2
    slack = jnp.where((donor == order[0]) | (sink == order[0]) | (tallies[sink] == 0), 0, jnp.maximum(slack, 0))
    shifted = jax.random.randint(jax.random.fold_in(own, 4), (count // 2,), 0, 1 << 20) % (slack + 1)
    tallies = tallies.at[donor].add(-shifted).at[sink].add(shifted)
    labels = jnp.searchsorted(jnp.cumsum(tallies), jnp.arange(rows * top), side="right").astype(jnp.int32)
    table = labels.reshape(top, rows).T
    table = table[jax.random.permutation(jax.random.fold_in(own, 1), rows)]
    offset_by = jax.random.randint(jax.random.fold_in(own, 2), (rows, 1), 0, top)
    return jnp.take_along_axis(table, (jnp.arange(top)[None, :] + offset_by) % top, axis=1)


def shares(amount, total, reach, skew, full):
    portions = [(1 << 20) // math.isqrt(rank ** skew) + 1 for rank in range(1, amount + 1)]
    largest = reach if full else min(reach, max(-(-total // amount), total * portions[0] // sum(portions)))
    least = 1 if total - largest >= amount - 1 else 0
    given, rest = [largest] + [least] * (amount - 1), total - largest - least * (amount - 1)
    while rest > 0:
        candidates = [i for i in range(1, amount) if given[i] < largest] or [i for i in range(1, amount) if given[i] < reach]
        whole, left = sum([portions[i] for i in candidates]), rest
        for i in candidates:
            more = min(reach - given[i], max(1, left * portions[i] // whole), rest)
            given[i] = given[i] + more
            rest = rest - more
    return np.array(given)


def scatter_about(stream_key, shape, spread, reach, split=(), held_as=jnp.bfloat16):
    drawn = spread * jax.random.normal(stream_key, shape, jnp.float32)
    if split:
        drawn = drawn * shard_levels(stream_key, shape, split, -0.22, 0.18)
    return jnp.clip(drawn, -reach, reach).astype(held_as)


def setup_inputs(seed: int = 0) -> dict:
    arg_keys = jax.random.split(jax.random.key(seed), 8)
    tokens = scatter_about(arg_keys[0], (TOKENS, D), 1.0, 6.0, ((0, 256), (1, 4)))
    out_grad = scatter_about(arg_keys[1], (TOKENS, D), 1.0, 6.0, ((0, 256), (1, 4)))
    expert_ids_keys = jax.random.split(jax.random.fold_in(arg_keys[2], 1), TOKENS // TOK_DEV)
    expert_ids_turns = jax.random.permutation(jax.random.fold_in(arg_keys[2], 3), TOKENS // TOK_DEV)
    expert_ids = jax.vmap(lambda own, number: shared_out(jax.random.fold_in(arg_keys[2], 2), own, number, TOK_DEV, EXPERTS, 2, CAP, 2))(expert_ids_keys, expert_ids_turns).reshape((TOKENS, 2))
    gate_probs = jnp.clip(0.1 + 0.9 * jax.random.uniform(arg_keys[3], (TOKENS, 2), jnp.float32) ** shard_levels(arg_keys[3], (TOKENS, 2), ((0, 256),), -0.2, 0.2), 0.1, 1.0)
    w_gate = scatter_about(arg_keys[4], (EXPERTS, D, HE), D ** -0.5, 0.09375, ((0, 16), (1, 4), (2, 16)))
    w_up = scatter_about(arg_keys[5], (EXPERTS, D, HE), D ** -0.5, 0.09375, ((0, 16), (1, 4), (2, 16)))
    w_down = scatter_about(arg_keys[6], (EXPERTS, HE, D), HE ** -0.5, 0.078125, ((0, 16), (1, 16), (2, 4)))
    return dict(tokens=tokens, out_grad=out_grad, expert_ids=expert_ids, gate_probs=gate_probs, w_gate=w_gate, w_up=w_up, w_down=w_down)


def slot_within(identity, experts):
    matches = (identity[:, :, None] == jnp.arange(experts, dtype=jnp.int32)[None, None, :]).astype(jnp.int32)
    before = jnp.cumsum(matches, axis=1) - matches
    return jnp.sum(before * matches, axis=2).astype(jnp.int32)


def expert_pass(operands):
    x_rows, dy_rows, gate_w, up_w, down_w = operands
    gate_sum = jnp.dot(x_rows, gate_w, preferred_element_type=jnp.float32)
    up_sum = jnp.dot(x_rows, up_w, preferred_element_type=jnp.float32)
    sigmoid_gate = jax.nn.sigmoid(gate_sum)
    swish_gate = gate_sum * sigmoid_gate
    hidden = (swish_gate * up_sum).astype(jnp.bfloat16)
    out_rows = jnp.dot(hidden, down_w, preferred_element_type=jnp.float32).astype(jnp.bfloat16)
    back_hidden = jnp.dot(dy_rows, down_w.T, preferred_element_type=jnp.float32)
    slope = sigmoid_gate * (1.0 + gate_sum * (1.0 - sigmoid_gate))
    grad_gate_rows = (back_hidden * up_sum * slope).astype(jnp.bfloat16)
    grad_up_rows = (back_hidden * swish_gate).astype(jnp.bfloat16)
    in_rows = (jnp.dot(grad_gate_rows, gate_w.T, preferred_element_type=jnp.float32)
               + jnp.dot(grad_up_rows, up_w.T, preferred_element_type=jnp.float32)).astype(jnp.bfloat16)
    gate_grad = jnp.dot(x_rows.T, grad_gate_rows, preferred_element_type=jnp.float32).astype(jnp.bfloat16)
    up_grad = jnp.dot(x_rows.T, grad_up_rows, preferred_element_type=jnp.float32).astype(jnp.bfloat16)
    down_grad = jnp.dot(hidden.T, dy_rows, preferred_element_type=jnp.float32).astype(jnp.bfloat16)
    return out_rows, in_rows, gate_grad, up_grad, down_grad


def reference(tokens, out_grad, expert_ids, gate_probs, w_gate, w_up, w_down):
    blocks = N_DP * N_EXPERT
    slot_total = blocks * CAP
    within = slot_within(expert_ids.reshape(blocks, TOK_DEV * 2), EXPERTS).reshape(-1)
    block_of = jnp.arange(TOKENS * 2, dtype=jnp.int32) // (TOK_DEV * 2)
    picked = expert_ids.reshape(-1).astype(jnp.int32)
    target = picked * slot_total + block_of * CAP + within
    source = jnp.arange(TOKENS * 2, dtype=jnp.int32) // 2
    total_slots = EXPERTS * slot_total
    owner_row = jnp.zeros((total_slots,), jnp.int32).at[target].set(source)
    filled = jnp.zeros((total_slots,), jnp.float32).at[target].set(1.0)
    weight_slot = jnp.zeros((total_slots,), jnp.float32).at[target].set(gate_probs.reshape(-1))
    x_slots = tokens[owner_row] * filled[:, None].astype(jnp.bfloat16)
    dy_slots = (weight_slot[:, None] * out_grad[owner_row].astype(jnp.float32)).astype(jnp.bfloat16)
    dims = (EXPERTS, slot_total, D)
    out_rows, in_rows, grad_gate, grad_up, grad_down = lax.map(
        expert_pass, (x_slots.reshape(dims), dy_slots.reshape(dims), w_gate, w_up, w_down))
    out_flat = out_rows.reshape(total_slots, D).astype(jnp.float32)
    in_flat = in_rows.reshape(total_slots, D).astype(jnp.float32)
    mixed = jnp.zeros((TOKENS, D), jnp.float32).at[owner_row].add(weight_slot[:, None] * out_flat)
    grad_tokens = jnp.zeros((TOKENS, D), jnp.float32).at[owner_row].add(filled[:, None] * in_flat)
    return (mixed.astype(jnp.bfloat16), grad_tokens.astype(jnp.bfloat16), grad_gate, grad_up, grad_down)
```

```python
import jax
import jax.numpy as jnp
from jax import lax
from jax.experimental import pallas as pl
from jax.experimental.pallas import tpu as pltpu
from jax.sharding import PartitionSpec as P

MESH = pl.DeviceIdType.MESH
BF = jnp.bfloat16
F32 = jnp.float32


def nn(a, b):
    return lax.dot_general(a, b, (((1,), (0,)), ((), ())), preferred_element_type=F32)


def nt(a, b):
    return lax.dot_general(a, b, (((1,), (1,)), ((), ())), preferred_element_type=F32)


def tn(a, b):
    return lax.dot_general(a, b, (((0,), (0,)), ((), ())), preferred_element_type=F32)


def flip(a):
    return a.astype(F32).T.astype(BF)


def kernel(
    tok_ref, og_ref, meta_ref, wg_ref, wu_ref, wd_ref,
    mixed_ref, gtok_ref, gg_ref, gu_ref, gd_ref,
    zed, sx, xd, ps, rp, hb, os_, ro, sb, rb, ts, rs, ta, ra,
    a_s, a_r, s_s, s_r, b_s, b_r, y_s, y_r, p_s, p_r, h_s, h_r,
    o_s, o_r, c_s, c_r, t_s, t_r, f_s, f_r,
):
    dp = lax.axis_index("dp")
    ex = lax.axis_index("expert")
    t = lax.axis_index("tp")
    zh, y, cl, c = dp // 4, dp % 4, ex // 2, ex % 2
    z = zh * 8 + cl
    sc = 1 - c

    def at_z(k):
        zz = (z + k + 32) % 32
        return ((zz // 8) * 4 + y, (zz % 8) * 2 + c, t)

    def at_y(yy):
        return (zh * 4 + yy, ex, t)

    def at_x(tt):
        return (dp, ex, tt)

    sib = (dp, cl * 2 + sc, t)

    def rdma(src, dst, ss, rr, to):
        return pltpu.make_async_remote_copy(
            src, dst, ss, rr, device_id=to, device_id_type=MESH
        )

    peers = [at_z(k) for k in (8, -8, 16, 1, -1, 2, -2, 3, -3, 4, -4)]
    peers += [sib]
    peers += [at_y((y + k) % 4) for k in (1, 2, 3)]
    peers += [at_x((t + k) % 4) for k in (1, 2, 3)]
    bar = pltpu.get_barrier_semaphore()
    for p in peers:
        pl.semaphore_signal(bar, inc=1, device_id=p, device_id_type=MESH)

    zed[zh, c, :, 0:896] = jnp.concatenate([tok_ref[...], og_ref[...]], axis=0)
    zed[zh, c, :, 896:1024] = meta_ref[...]
    pl.semaphore_wait(bar, len(peers))

    pend = []

    def go(copy):
        copy.start()
        pend.append(copy)
        return copy

    ac = {}
    for k in (2, 1, 3):
        me = zed.at[zh, c]
        ac[k] = go(rdma(me, me, a_s.at[k], a_r.at[k], at_z(8 * k)))
    sc_copies = []
    for k in (0, 1, 3, 2):
        src = (zh + 4 - k) % 4
        if k:
            ac[k].wait_recv()
        blk = zed.at[src, c]
        sc_copies.append(go(rdma(blk, blk, s_s.at[k], s_r.at[k], sib)))
    for q in sc_copies:
        q.wait_recv()

    meta = jnp.zeros((16, 128), F32)
    for j in range(4):
        for cc in range(2):
            meta = meta + zed[j, cc, :, 896:1024].astype(F32)
    rid = (lax.broadcasted_iota(jnp.int32, (128, 128), 0) + 1 + 128 * c).astype(F32)
    first = rid == meta[0:1, :]
    second = rid == meta[1:2, :]
    one = jnp.where(first | second, 1.0, 0.0)
    weights = [
        jnp.where(first, meta[2 + i : 3 + i, :], 0.0)
        + jnp.where(second, meta[5 + i : 6 + i, :], 0.0)
        for i in range(3)
    ]
    is_tok = (lax.broadcasted_iota(jnp.int32, (128, 128), 1) % 16) < 8
    rows = zed[:, :, :, 0:896].reshape(128, 896)
    x_slots = nn(jnp.where(is_tok, one, 0.0).astype(BF), rows).astype(BF)
    dy_slots = sum(nn(jnp.where(is_tok, 0.0, w).astype(BF), rows) for w in weights)
    dy_slots = dy_slots.astype(BF)
    sx[0] = x_slots.reshape(8, 16, 896)
    sx[1] = dy_slots.reshape(8, 16, 896)

    def window(src, dst, ss, rr):
        got = []
        for i, k in enumerate((3, -3, 2, -2, 1, -1)):
            to = (cl + k + 8) % 8
            got.append(
                go(rdma(src.at[:, to], dst(slice(None)), ss.at[i], rr.at[i], at_z(k)))
            )
        to = (cl + 4) % 8
        got.append(go(rdma(src.at[0, to], dst(0), ss.at[6], rr.at[6], at_z(4))))
        got.append(go(rdma(src.at[1, to], dst(1), ss.at[7], rr.at[7], at_z(-4))))
        return got

    got = window(sx, lambda a: xd.at[y, a, cl], b_s, b_r)
    xd[y, :, cl] = sx[:, cl]
    for q in got:
        q.wait_recv()

    left, right = (y + 3) % 4, (y + 1) % 4
    yc = {}
    for a, d in ((0, 0), (1, 1), (1, 0), (0, 1)):
        blk = xd.at[y, a]
        i = a * 2 + d
        yc[a, d] = go(rdma(blk, blk, y_s.at[i], y_r.at[i], at_y(left if d else right)))

    def half(yy):
        x = xd[yy, 0].reshape(128, 896)
        d = xd[yy, 1].reshape(128, 896)
        ps[yy, 0] = nn(x, wg_ref[0]).T.astype(BF)
        ps[yy, 1] = nn(x, wu_ref[0]).T.astype(BF)
        ps[yy, 2] = nt(d, wd_ref[0]).T.astype(BF)
        k = (yy - t + 4) % 4

        @pl.when(k != 0)
        def _():
            rdma(ps.at[yy], rp.at[t], p_s.at[k], p_r.at[k], at_x(yy)).start()

    half(y)
    yc[0, 0].wait_recv()
    blk = xd.at[left, 0]
    f0 = go(rdma(blk, blk, y_s.at[4], y_r.at[4], at_y(right)))
    yc[1, 1].wait_recv()
    blk = xd.at[right, 1]
    f1 = go(rdma(blk, blk, y_s.at[5], y_r.at[5], at_y(left)))
    yc[1, 0].wait_recv()
    half(left)
    yc[0, 1].wait_recv()
    half(right)
    f0.wait_recv()
    f1.wait_recv()
    half((y + 2) % 4)

    g = ps[t, 0].astype(F32)
    u = ps[t, 1].astype(F32)
    b = ps[t, 2].astype(F32)
    for k in (1, 3, 2):
        src = (t + 4 - k) % 4
        q = rdma(ps.at[src], rp.at[src], p_s.at[k], p_r.at[k], at_x((t + k) % 4))
        q.wait()
        g = g + rp[src, 0].astype(F32)
        u = u + rp[src, 1].astype(F32)
        b = b + rp[src, 2].astype(F32)
    s = jax.nn.sigmoid(g)
    sw = g * s
    hb[t, 0] = (sw * u).astype(BF)
    hb[t, 1] = (b * u * (s * (1.0 + g * (1.0 - s)))).astype(BF)
    hb[t, 2] = (b * sw).astype(BF)
    hc = {}
    for k in (2, 1, 3):
        blk = hb.at[t]
        hc[k] = go(rdma(blk, blk, h_s.at[k], h_r.at[k], at_x((t + k) % 4)))

    def back(j):
        os_[j, 0] = nn(flip(hb[j, 0]), wd_ref[0]).astype(BF)
        os_[j, 1] = (
            nt(flip(hb[j, 1]), wg_ref[0]) + nt(flip(hb[j, 2]), wu_ref[0])
        ).astype(BF)
        k = (j - y + 4) % 4

        @pl.when(k != 0)
        def _():
            rdma(os_.at[j], ro.at[y], o_s.at[k], o_r.at[k], at_y(j)).start()

    back(t)
    for k in (1, 3, 2):
        hc[k].wait_recv()
        back((t + 4 - k) % 4)

    for i, out in ((1, gg_ref), (2, gu_ref)):
        acc = sum(nn(hb[j, i], xd[j, 0].reshape(128, 896)) for j in range(4))
        out[0] = acc.T.astype(BF)
    acc = sum(nn(hb[j, 0], xd[j, 1].reshape(128, 896)) for j in range(4))
    gd_ref[0] = acc.astype(BF)

    acc = [os_[y, 0].astype(F32), os_[y, 1].astype(F32)]
    for k in (1, 3, 2):
        src = (y + 4 - k) % 4
        q = rdma(os_.at[src], ro.at[src], o_s.at[k], o_r.at[k], at_y((y + k) % 4))
        q.wait()
        acc = [acc[i] + ro[src, i].astype(F32) for i in range(2)]
    for i in range(2):
        sb[i] = acc[i].astype(BF).reshape(8, 16, 896)

    got = window(sb, lambda a: rb.at[a, cl], c_s, c_r)
    rb[:, cl] = sb[:, cl]
    for q in got:
        q.wait_recv()
    r0 = rb[0].reshape(128, 896)
    r1 = rb[1].reshape(128, 896)
    tot = nn(jnp.where(is_tok, 0.0, one).T.astype(BF), r1)
    for w in weights:
        tot = tot + nn(jnp.where(is_tok, w, 0.0).T.astype(BF), r0)
    ta[...] = tot.reshape(4, 2, 16, 896)
    ts[...] = ta[:, sc].astype(BF)
    q = go(rdma(ts, rs, t_s, t_r, sib))
    q.wait_recv()
    part = ta[:, c] + rs[...].astype(F32)
    ta[:, c] = part
    ts2 = part.astype(BF)
    ra[4:8] = ts2
    fc = {}
    for k in (2, 1, 3):
        fc[k] = go(
            rdma(ra.at[4 + (zh + k) % 4], ra.at[k], f_s.at[k], f_r.at[k], at_z(8 * k))
        )
    fin = ta[zh, c]
    for k in (1, 3, 2):
        fc[k].wait_recv()
        fin = fin + ra[k].astype(F32)
    fin = fin.astype(BF)
    mixed_ref[...] = fin[0:8]
    gtok_ref[...] = fin[8:16]

    for q in pend:
        q.wait_send()


def routing(expert_ids, gate_probs):
    zh = lax.axis_index("dp") // 4
    c = lax.axis_index("expert") % 2
    flat = expert_ids.reshape(16)
    earlier = jnp.arange(16)[None, :] < jnp.arange(16)[:, None]
    rank = jnp.sum((flat[:, None] == flat[None, :]) & earlier, axis=1).reshape(8, 2)
    slot = (expert_ids // 2) * 16 + zh * 4 + c * 2 + rank + 128 * (expert_ids % 2) + 1
    hi = lax.reduce_precision(gate_probs, 8, 7)
    rest = gate_probs - hi
    mid = lax.reduce_precision(rest, 8, 7)
    low = rest - mid
    table = jnp.stack(
        [slot[:, 0].astype(F32), slot[:, 1].astype(F32)]
        + [part[:, i] for i in range(2) for part in (hi, mid, low)]
    )
    table = jnp.concatenate([table, table], axis=1)
    table = jnp.pad(table, ((0, 8), (0, 0)))
    here = (jnp.arange(128) // 16) == (zh * 2 + c)
    return jnp.where(here[None, :], jnp.tile(table, (1, 8)), 0.0).astype(BF)


def shards(tokens, out_grad, expert_ids, gate_probs, w_gate, w_up, w_down):
    meta = routing(expert_ids, gate_probs)
    vm = pl.BlockSpec(memory_space=pltpu.VMEM)
    dma = pltpu.SemaphoreType.DMA
    return pl.pallas_call(
        kernel,
        out_shape=(
            jax.ShapeDtypeStruct((8, 896), BF),
            jax.ShapeDtypeStruct((8, 896), BF),
            jax.ShapeDtypeStruct((1, 896, 304), BF),
            jax.ShapeDtypeStruct((1, 896, 304), BF),
            jax.ShapeDtypeStruct((1, 304, 896), BF),
        ),
        in_specs=[vm] * 6,
        out_specs=(vm,) * 5,
        scratch_shapes=[
            pltpu.VMEM((4, 2, 16, 1024), BF),
            pltpu.VMEM((2, 8, 16, 896), BF),
            pltpu.VMEM((4, 2, 8, 16, 896), BF),
            pltpu.VMEM((4, 3, 304, 128), BF),
            pltpu.VMEM((4, 3, 304, 128), BF),
            pltpu.VMEM((4, 3, 304, 128), BF),
            pltpu.VMEM((4, 2, 128, 896), BF),
            pltpu.VMEM((4, 2, 128, 896), BF),
            pltpu.VMEM((2, 8, 16, 896), BF),
            pltpu.VMEM((2, 8, 16, 896), BF),
            pltpu.VMEM((4, 16, 896), BF),
            pltpu.VMEM((4, 16, 896), BF),
            pltpu.VMEM((4, 2, 16, 896), F32),
            pltpu.VMEM((8, 16, 896), BF),
        ]
        + [dma((4,))] * 4
        + [dma((8,))] * 4
        + [dma((4,))] * 6
        + [dma((8,))] * 2
        + [dma, dma]
        + [dma((4,))] * 2,
        compiler_params=pltpu.CompilerParams(
            collective_id=0, has_side_effects=True, vmem_limit_bytes=48 << 20
        ),
        cost_estimate=pl.CostEstimate(
            flops=2600000000, bytes_accessed=4000000, transcendentals=40000
        ),
    )(tokens, out_grad, meta, w_gate, w_up, w_down)


def solution(mesh):
    wide = P(("dp", "expert"), "tp")
    rows = P(("dp", "expert"), None)
    up = P("expert", "tp", "dp")
    down = P("expert", "dp", "tp")
    return jax.shard_map(
        shards,
        mesh=mesh,
        in_specs=(wide, wide, rows, rows, up, up, down),
        out_specs=(wide, wide, up, up, down),
        check_vma=False,
    )
```

```python
import jax
import jax.numpy as jnp
from jax import lax
from jax.experimental import pallas as pl
from jax.experimental.pallas import tpu as pltpu
from jax.sharding import PartitionSpec as P

MESH = pl.DeviceIdType.MESH
BF = jnp.bfloat16
F32 = jnp.float32


def nn(a, b):
    return lax.dot_general(a, b, (((1,), (0,)), ((), ())), preferred_element_type=F32)


def nt(a, b):
    return lax.dot_general(a, b, (((1,), (1,)), ((), ())), preferred_element_type=F32)


def tn(a, b):
    return lax.dot_general(a, b, (((0,), (0,)), ((), ())), preferred_element_type=F32)


OFFS = (4, 3, -3, 2, -2, 1, -1)


def kernel(
    tok_ref, og_ref, meta_ref, wg_ref, wu_ref, wd_ref,
    mixed_ref, gtok_ref, gg_ref, gu_ref, gd_ref,
    w, zed, sx, xd, ps, rp, hb, os_, ro, sb, rb, ts, rs, ta, ra, gr,
    a_s, a_r, s_s, s_r, b_s, b_r, y_s, y_r, v_s, v_r, p_s, p_r, h_s, h_r,
    o_s, o_r, c_s, c_r, t_s, t_r, f_s, f_r, w_m, g_m,
):
    dp = lax.axis_index("dp")
    ex = lax.axis_index("expert")
    t = lax.axis_index("tp")
    zh, y, cl, c = dp // 4, dp % 4, ex // 2, ex % 2
    z = zh * 8 + cl
    sc = 1 - c

    def at_z(k):
        zz = (z + k + 32) % 32
        return ((zz // 8) * 4 + y, (zz % 8) * 2 + c, t)

    def at_y(yy):
        return (zh * 4 + yy, ex, t)

    def at_x(tt):
        return (dp, ex, tt)

    def klass(k):
        return (cl + k + 8) % 8

    sib = (dp, cl * 2 + sc, t)

    def rdma(src, dst, ss, rr, to):
        return pltpu.make_async_remote_copy(
            src, dst, ss, rr, device_id=to, device_id_type=MESH
        )

    peers = [at_z(k) for k in (16, 8, -8, 4, -4, 3, -3, 2, -2, 1, -1)]
    peers += [at_y((y + k) % 4) for k in (1, 2, 3)]
    peers += [at_x((t + k) % 4) for k in (1, 2, 3)]
    peers += [sib]
    bar = pltpu.get_barrier_semaphore()
    for p in peers:
        pl.semaphore_signal(bar, inc=1, device_id=p, device_id_type=MESH)

    zed[zh, c, :, 0:896] = jnp.concatenate([tok_ref[...], og_ref[...]], axis=0)
    zed[zh, c, :, 896:1024] = meta_ref[...]
    loads = []
    for i, (ref, at) in enumerate(((wg_ref, 0), (wu_ref, 304), (wd_ref, 640))):
        q = pltpu.make_async_copy(ref.at[0], w.at[pl.ds(at, 304)], w_m.at[i])
        q.start()
        loads.append(q)
    w[608:640] = jnp.zeros((32, 896), BF)
    w[944:1024] = jnp.zeros((80, 896), BF)
    pl.semaphore_wait(bar, len(peers))

    pend = []

    def go(copy):
        copy.start()
        pend.append(copy)
        return copy

    ac = {}
    for k in (2, 1, 3):
        me = zed.at[zh, c]
        ac[k] = go(rdma(me, me, a_s.at[k], a_r.at[k], at_z(8 * k)))
    sc_copies = []
    for k in (0, 1, 3, 2):
        src = (zh + 4 - k) % 4
        if k:
            ac[k].wait_recv()
        blk = zed.at[src, c]
        sc_copies.append(go(rdma(blk, blk, s_s.at[k], s_r.at[k], sib)))
    for q in sc_copies:
        q.wait_recv()

    meta = jnp.zeros((16, 128), F32)
    for j in range(4):
        for cc in range(2):
            meta = meta + zed[j, cc, :, 896:1024].astype(F32)
    rid = (lax.broadcasted_iota(jnp.int32, (128, 128), 0) + 1 + 128 * c).astype(F32)
    first = rid == meta[0:1, :]
    second = rid == meta[1:2, :]
    one = jnp.where(first | second, 1.0, 0.0)
    weights = [
        jnp.where(first, meta[2 + i : 3 + i, :], 0.0)
        + jnp.where(second, meta[5 + i : 6 + i, :], 0.0)
        for i in range(3)
    ]
    is_tok = (lax.broadcasted_iota(jnp.int32, (128, 128), 1) % 16) < 8
    rows = zed[:, :, :, 0:896].reshape(128, 896)
    x_slots = nn(jnp.where(is_tok, one, 0.0).astype(BF), rows).astype(BF)
    dy_slots = sum(nn(jnp.where(is_tok, 0.0, m).astype(BF), rows) for m in weights)
    dy_slots = dy_slots.astype(BF)
    sx[0] = x_slots.reshape(8, 16, 896)
    sx[1] = dy_slots.reshape(8, 16, 896)

    def near(src, dst, ss, rr, i):
        k = OFFS[i]
        to = klass(k)
        if i:
            return [go(rdma(src.at[:, to], dst(slice(None)), ss.at[i], rr.at[i], at_z(k)))]
        return [
            go(rdma(src.at[0, to], dst(0), ss.at[0], rr.at[0], at_z(4))),
            go(rdma(src.at[1, to], dst(1), ss.at[7], rr.at[7], at_z(-4))),
        ]

    got = {i: near(sx, lambda a: xd.at[y, a, cl], b_s, b_r, i) for i in range(7)}
    xd[y, :, cl] = sx[:, cl]

    left, right = (y + 3) % 4, (y + 1) % 4
    yc = []
    for i in (7, 5, 6, 3, 4, 1, 2, 0):
        src = cl if i == 7 else klass(-OFFS[i])
        if i < 7:
            for q in got[i]:
                q.wait_recv()
        blk = xd.at[y, :, src]
        yc.append(
            (
                src,
                i,
                go(rdma(blk, blk, y_s.at[0, i], y_r.at[0, i], at_y(right))),
                go(rdma(blk, blk, y_s.at[1, i], y_r.at[1, i], at_y(left))),
            )
        )
    for q in loads:
        q.wait()

    chunks = (y, left, right, (y + 2) % 4)

    def half(m):
        yy = chunks[m]
        gu = nt(xd[yy, 0].reshape(128, 896), w[0:640])
        b = nt(xd[yy, 1].reshape(128, 896), w[640:1024])
        ps[m, :, :, 0:640] = gu.astype(BF).reshape(4, 32, 640)
        ps[m, :, :, 640:1024] = b.astype(BF).reshape(4, 32, 384)
        for k in (2, 1, 3):
            q = (t + k) % 4
            go(rdma(ps.at[m, q], rp.at[m, k], p_s.at[m, k], p_r.at[m, k], at_x(q)))

    def middle(m):
        acc = ps[m, t].astype(F32)
        for k in (1, 3, 2):
            ref = rp.at[m, k]
            rdma(ref, ref, p_s.at[m, k], p_r.at[m, k], at_x((t + k) % 4)).wait_recv()
            acc = acc + rp[m, k].astype(F32)
        g, u, b = acc[:, 0:304], acc[:, 304:608], acc[:, 640:944]
        s = jax.nn.sigmoid(g)
        sw = g * s
        hb[m, t] = jnp.concatenate(
            [
                b * u * (s * (1.0 + g * (1.0 - s))),
                b * sw,
                jnp.zeros((32, 32), F32),
                sw * u,
                jnp.zeros((32, 80), F32),
            ],
            axis=1,
        ).astype(BF)
        for k in (2, 1, 3):
            blk = hb.at[m, t]
            go(rdma(blk, blk, h_s.at[m, k], h_r.at[m, k], at_x((t + k) % 4)))

    def back(m):
        for k in (1, 3, 2):
            blk = hb.at[m, (t + 4 - k) % 4]
            rdma(blk, blk, h_s.at[m, k], h_r.at[m, k], at_x((t + k) % 4)).wait_recv()
        h = hb[m].reshape(128, 1024)
        os_[m, 0] = nn(h[:, 640:1024], w[640:1024]).astype(BF).reshape(8, 16, 896)
        os_[m, 1] = nn(h[:, 0:640], w[0:640]).astype(BF).reshape(8, 16, 896)
        if m:
            for i in range(8):
                to = cl if i == 7 else klass(OFFS[i])
                go(
                    rdma(
                        os_.at[m, :, to], ro.at[m, :, to],
                        o_s.at[m, i], o_r.at[m, i], at_y(chunks[m]),
                    )
                )

    half(0)
    fw = []
    for src, i, to_right, to_left in yc:
        to_right.wait_recv()
        blk = xd.at[left, 0, src]
        fw.append(go(rdma(blk, blk, v_s.at[0, i], v_r.at[0, i], at_y(right))))
        to_left.wait_recv()
        blk = xd.at[right, 1, src]
        fw.append(go(rdma(blk, blk, v_s.at[1, i], v_r.at[1, i], at_y(left))))
    half(1)
    half(2)
    middle(0)
    for q in fw:
        q.wait_recv()
    half(3)
    middle(1)
    middle(2)
    back(0)
    back(1)
    back(2)
    middle(3)
    back(3)

    order = [xd[chunks[m], 0].reshape(128, 896) for m in range(4)]
    xs = jnp.concatenate(order, axis=0)
    ds = jnp.concatenate([xd[chunks[m], 1].reshape(128, 896) for m in range(4)], axis=0)
    hs = hb[...].reshape(512, 1024)
    for at, n, r in ((0, 256, xs), (256, 256, xs), (512, 128, xs), (640, 384, ds)):
        gr[at : at + n] = tn(hs[:, at : at + n], r).astype(BF)
    saves = []
    for i, (ref, at) in enumerate(((gg_ref, 0), (gu_ref, 304), (gd_ref, 640))):
        q = pltpu.make_async_copy(gr.at[pl.ds(at, 304)], ref.at[0], g_m.at[i])
        q.start()
        saves.append(q)

    got = []
    for i in range(8):
        to = cl if i == 7 else klass(OFFS[i])
        acc = os_[0, :, to].astype(F32)
        for m in (1, 2, 3):
            ref = ro.at[m, :, to]
            rdma(ref, ref, o_s.at[m, i], o_r.at[m, i], at_y(chunks[m])).wait_recv()
            acc = acc + ro[m, :, to].astype(F32)
        if i == 7:
            rb[:, cl] = acc.astype(BF)
        else:
            sb[:, to] = acc.astype(BF)
            got += near(sb, lambda a: rb.at[a, cl], c_s, c_r, i)
    for q in got:
        q.wait_recv()

    r0 = rb[0].reshape(128, 896)
    r1 = rb[1].reshape(128, 896)
    tot = nn(jnp.where(is_tok, 0.0, one).T.astype(BF), r1)
    for m in weights:
        tot = tot + nn(jnp.where(is_tok, m, 0.0).T.astype(BF), r0)
    ta[...] = tot.reshape(4, 2, 16, 896)
    ts[...] = ta[:, sc].astype(BF)
    go(rdma(ts, rs, t_s, t_r, sib)).wait_recv()
    part = ta[:, c] + rs[...].astype(F32)
    ta[:, c] = part
    ra[4:8] = part.astype(BF)
    fc = {}
    for k in (2, 1, 3):
        fc[k] = go(
            rdma(ra.at[4 + (zh + k) % 4], ra.at[k], f_s.at[k], f_r.at[k], at_z(8 * k))
        )
    fin = ta[zh, c]
    for k in (1, 3, 2):
        fc[k].wait_recv()
        fin = fin + ra[k].astype(F32)
    fin = fin.astype(BF)
    mixed_ref[...] = fin[0:8]
    gtok_ref[...] = fin[8:16]

    for q in pend:
        q.wait_send()
    for q in saves:
        q.wait()


def routing(expert_ids, gate_probs):
    zh = lax.axis_index("dp") // 4
    c = lax.axis_index("expert") % 2
    flat = expert_ids.reshape(16)
    earlier = jnp.arange(16)[None, :] < jnp.arange(16)[:, None]
    rank = jnp.sum((flat[:, None] == flat[None, :]) & earlier, axis=1).reshape(8, 2)
    slot = (expert_ids // 2) * 16 + zh * 4 + c * 2 + rank + 128 * (expert_ids % 2) + 1
    hi = lax.reduce_precision(gate_probs, 8, 7)
    rest = gate_probs - hi
    mid = lax.reduce_precision(rest, 8, 7)
    low = rest - mid
    table = jnp.stack(
        [slot[:, 0].astype(F32), slot[:, 1].astype(F32)]
        + [part[:, i] for i in range(2) for part in (hi, mid, low)]
    )
    table = jnp.concatenate([table, table], axis=1)
    table = jnp.pad(table, ((0, 8), (0, 0)))
    here = (jnp.arange(128) // 16) == (zh * 2 + c)
    return jnp.where(here[None, :], jnp.tile(table, (1, 8)), 0.0).astype(BF)


def shards(tokens, out_grad, expert_ids, gate_probs, w_gate, w_up, w_down):
    meta = routing(expert_ids, gate_probs)
    vm = pl.BlockSpec(memory_space=pltpu.VMEM)
    hbm = pl.BlockSpec(memory_space=pl.ANY)
    dma = pltpu.SemaphoreType.DMA
    mixed, gtok, gg, gu, gd = pl.pallas_call(
        kernel,
        out_shape=(
            jax.ShapeDtypeStruct((8, 896), BF),
            jax.ShapeDtypeStruct((8, 896), BF),
            jax.ShapeDtypeStruct((1, 304, 896), BF),
            jax.ShapeDtypeStruct((1, 304, 896), BF),
            jax.ShapeDtypeStruct((1, 304, 896), BF),
        ),
        in_specs=[vm] * 3 + [hbm] * 3,
        out_specs=(vm,) * 2 + (hbm,) * 3,
        scratch_shapes=[
            pltpu.VMEM((1024, 896), BF),
            pltpu.VMEM((4, 2, 16, 1024), BF),
            pltpu.VMEM((2, 8, 16, 896), BF),
            pltpu.VMEM((4, 2, 8, 16, 896), BF),
            pltpu.VMEM((4, 4, 32, 1024), BF),
            pltpu.VMEM((4, 4, 32, 1024), BF),
            pltpu.VMEM((4, 4, 32, 1024), BF),
            pltpu.VMEM((4, 2, 8, 16, 896), BF),
            pltpu.VMEM((4, 2, 8, 16, 896), BF),
            pltpu.VMEM((2, 8, 16, 896), BF),
            pltpu.VMEM((2, 8, 16, 896), BF),
            pltpu.VMEM((4, 16, 896), BF),
            pltpu.VMEM((4, 16, 896), BF),
            pltpu.VMEM((4, 2, 16, 896), F32),
            pltpu.VMEM((8, 16, 896), BF),
            pltpu.VMEM((1024, 896), BF),
        ]
        + [dma((4,))] * 4
        + [dma((8,))] * 2
        + [dma((2, 8))] * 4
        + [dma((4, 4))] * 4
        + [dma((4, 8))] * 2
        + [dma((8,))] * 2
        + [dma, dma]
        + [dma((4,))] * 2
        + [dma((3,))] * 2,
        compiler_params=pltpu.CompilerParams(
            collective_id=0, has_side_effects=True, vmem_limit_bytes=48 << 20
        ),
        cost_estimate=pl.CostEstimate(
            flops=2600000000, bytes_accessed=4000000, transcendentals=40000
        ),
    )(
        tokens, out_grad, meta,
        w_gate.transpose(0, 2, 1), w_up.transpose(0, 2, 1), w_down,
    )
    return mixed, gtok, gg.transpose(0, 2, 1), gu.transpose(0, 2, 1), gd


def solution(mesh):
    wide = P(("dp", "expert"), "tp")
    rows = P(("dp", "expert"), None)
    up = P("expert", "tp", "dp")
    down = P("expert", "dp", "tp")
    return jax.shard_map(
        shards,
        mesh=mesh,
        in_specs=(wide, wide, rows, rows, up, up, down),
        out_specs=(wide, wide, up, up, down),
        check_vma=False,
    )
```

```python
import jax
import jax.numpy as jnp
from jax import lax
from jax.experimental import pallas as pl
from jax.experimental.pallas import tpu as pltpu
from jax.sharding import PartitionSpec as P

MESH = pl.DeviceIdType.MESH
BF = jnp.bfloat16
F32 = jnp.float32


def nn(a, b):
    return lax.dot_general(a, b, (((1,), (0,)), ((), ())), preferred_element_type=F32)


def nt(a, b):
    return lax.dot_general(a, b, (((1,), (1,)), ((), ())), preferred_element_type=F32)


def tn(a, b):
    return lax.dot_general(a, b, (((0,), (0,)), ((), ())), preferred_element_type=F32)


OFFS = (4, 3, -3, 2, -2, 1, -1)


def routing(ids, probs, zh, c):
    rank = jnp.zeros((2, 8), jnp.int32)
    for d in range(1, 8):
        before = jnp.concatenate([jnp.full((2, d), -1, jnp.int32), ids[:, : 8 - d]], axis=1)
        same = (ids == before[0:1]) | (ids == before[1:2])
        rank = rank + jnp.where(same, 1, 0)
    slot = (ids >> 1) * 16 + (ids & 1) * 128 + rank + (zh * 4 + c * 2 + 1)
    slot = slot.astype(F32)
    hi = probs.astype(BF).astype(F32)
    mid = (probs - hi).astype(BF).astype(F32)
    low = probs - hi - mid
    table = [slot] + [part[i : i + 1] for i in range(2) for part in (hi, mid, low)]
    table = jnp.concatenate(table, axis=0)
    table = jnp.concatenate([table] * 16, axis=1)
    here = (lax.broadcasted_iota(jnp.int32, (8, 128), 1) // 16) == (zh * 2 + c)
    table = jnp.where(here, table, 0.0)
    return jnp.concatenate([table, jnp.zeros((8, 128), F32)], axis=0).astype(BF)


def kernel(
    tok_ref, og_ref, ids_ref, probs_ref, wg_ref, wu_ref, wd_ref,
    mixed_ref, gtok_ref, gg_ref, gu_ref, gd_ref,
    w, zed, sx, xd, ps, rp, hb, os_, ro, sb, rb, ts, rs, fs, f1, fg, f2, gr,
    a_s, a_r, s_s, s_r, b_s, b_r, y_s, y_r, v_s, v_r, p_s, p_r, h_s, h_r,
    o_s, o_r, c_s, c_r, t_s, t_r, f_s, f_r, w_m,
):
    dp = lax.axis_index("dp")
    ex = lax.axis_index("expert")
    t = lax.axis_index("tp")
    zh, y, cl, c = dp // 4, dp % 4, ex // 2, ex % 2
    z = zh * 8 + cl
    sc = 1 - c

    def at_z(k):
        zz = (z + k + 32) % 32
        return ((zz // 8) * 4 + y, (zz % 8) * 2 + c, t)

    def at_y(yy):
        return (zh * 4 + yy, ex, t)

    def at_x(tt):
        return (dp, ex, tt)

    def klass(k):
        return (cl + k + 8) % 8

    sib = (dp, cl * 2 + sc, t)

    def rdma(src, dst, ss, rr, to):
        return pltpu.make_async_remote_copy(
            src, dst, ss, rr, device_id=to, device_id_type=MESH
        )

    peers = [at_z(k) for k in (8, -8, 4, -4, 3, -3, 2, -2, 1, -1)]
    peers += [at_y((y + k) % 4) for k in (1, 2, 3)]
    peers += [at_x((t + k) % 4) for k in (1, 2, 3)]
    peers += [sib]
    bar = pltpu.get_barrier_semaphore()
    for p in peers:
        pl.semaphore_signal(bar, inc=1, device_id=p, device_id_type=MESH)

    zed[zh, c, :, 0:896] = jnp.concatenate([tok_ref[...], og_ref[...]], axis=0)
    zed[zh, c, :, 896:1024] = routing(ids_ref[...], probs_ref[...], zh, c)
    loads = []
    for i, (ref, at) in enumerate(((wg_ref, 0), (wu_ref, 304), (wd_ref, 640))):
        q = pltpu.make_async_copy(ref.at[0], w.at[pl.ds(at, 304)], w_m.at[i])
        q.start()
        loads.append(q)
    w[608:640] = jnp.zeros((32, 896), BF)
    w[944:1024] = jnp.zeros((80, 896), BF)
    pl.semaphore_wait(bar, len(peers))

    pend = []

    def go(copy):
        copy.start()
        pend.append(copy)
        return copy

    up, down = at_z(8), at_z(-8)
    zr, zl, zo = (zh + 1) % 4, (zh + 3) % 4, (zh + 2) % 4
    halves = (pl.ds(0, 512), pl.ds(512, 512))

    def along(who, h, i, to):
        blk = zed.at[who, c, :, halves[h]]
        return go(rdma(blk, blk, a_s.at[i], a_r.at[i], to))

    ac = [along(zh, i // 2 ^ i % 2, i, (up, down)[i % 2]) for i in range(4)]
    sc_copies = []

    def across(who):
        blk = zed.at[who, c]
        i = len(sc_copies)
        sc_copies.append(go(rdma(blk, blk, s_s.at[i], s_r.at[i], sib)))

    across(zh)
    ac[0].wait_recv()
    ac.append(along(zl, 0, 4, up))
    ac[1].wait_recv()
    ac.append(along(zr, 1, 5, down))
    ac[2].wait_recv()
    across(zl)
    ac[3].wait_recv()
    across(zr)
    ac[4].wait_recv()
    ac[5].wait_recv()
    across(zo)
    for q in sc_copies:
        q.wait_recv()

    meta = jnp.zeros((16, 128), F32)
    for j in range(4):
        for cc in range(2):
            meta = meta + zed[j, cc, :, 896:1024].astype(F32)
    rid = (lax.broadcasted_iota(jnp.int32, (128, 128), 0) + 1 + 128 * c).astype(F32)
    first = rid == meta[0:1, :]
    second = rid == meta[1:2, :]
    one = jnp.where(first | second, 1.0, 0.0)
    weights = [
        jnp.where(first, meta[2 + i : 3 + i, :], 0.0)
        + jnp.where(second, meta[5 + i : 6 + i, :], 0.0)
        for i in range(3)
    ]
    is_tok = (lax.broadcasted_iota(jnp.int32, (128, 128), 1) % 16) < 8
    rows = zed[:, :, :, 0:896].reshape(128, 896)
    x_slots = nn(jnp.where(is_tok, one, 0.0).astype(BF), rows).astype(BF)
    dy_slots = sum(nn(jnp.where(is_tok, 0.0, m).astype(BF), rows) for m in weights)
    dy_slots = dy_slots.astype(BF)
    sx[0] = x_slots.reshape(8, 16, 896)
    sx[1] = dy_slots.reshape(8, 16, 896)

    def near(src, dst, ss, rr, i):
        k = OFFS[i]
        to = klass(k)
        if i:
            return [go(rdma(src.at[:, to], dst(slice(None)), ss.at[i], rr.at[i], at_z(k)))]
        return [
            go(rdma(src.at[0, to], dst(0), ss.at[0], rr.at[0], at_z(4))),
            go(rdma(src.at[1, to], dst(1), ss.at[7], rr.at[7], at_z(-4))),
        ]

    got = {i: near(sx, lambda a: xd.at[y, a, cl], b_s, b_r, i) for i in range(7)}
    xd[y, :, cl] = sx[:, cl]

    left, right = (y + 3) % 4, (y + 1) % 4
    yc = []
    for i in (7, 5, 6, 3, 4, 1, 2, 0):
        src = cl if i == 7 else klass(-OFFS[i])
        if i < 7:
            for q in got[i]:
                q.wait_recv()
        blk = xd.at[y, :, src]
        yc.append(
            (
                src,
                i,
                go(rdma(blk, blk, y_s.at[0, i], y_r.at[0, i], at_y(right))),
                go(rdma(blk, blk, y_s.at[1, i], y_r.at[1, i], at_y(left))),
            )
        )
    for q in loads:
        q.wait()

    chunks = (y, left, right, (y + 2) % 4)

    def half(m):
        yy = chunks[m]
        gu = nt(xd[yy, 0].reshape(128, 896), w[0:640])
        b = nt(xd[yy, 1].reshape(128, 896), w[640:1024])
        ps[m, :, :, 0:640] = gu.astype(BF).reshape(4, 32, 640)
        ps[m, :, :, 640:1024] = b.astype(BF).reshape(4, 32, 384)
        for k in (2, 1, 3):
            q = (t + k) % 4
            go(rdma(ps.at[m, q], rp.at[m, k], p_s.at[m, k], p_r.at[m, k], at_x(q)))

    def middle(m):
        acc = ps[m, t].astype(F32)
        for k in (1, 3, 2):
            ref = rp.at[m, k]
            rdma(ref, ref, p_s.at[m, k], p_r.at[m, k], at_x((t + k) % 4)).wait_recv()
            acc = acc + rp[m, k].astype(F32)
        g, u, b = acc[:, 0:304], acc[:, 304:608], acc[:, 640:944]
        s = jax.nn.sigmoid(g)
        sw = g * s
        hb[m, t] = jnp.concatenate(
            [
                b * u * (s * (1.0 + g * (1.0 - s))),
                b * sw,
                jnp.zeros((32, 32), F32),
                sw * u,
                jnp.zeros((32, 80), F32),
            ],
            axis=1,
        ).astype(BF)
        for k in (2, 1, 3):
            blk = hb.at[m, t]
            go(rdma(blk, blk, h_s.at[m, k], h_r.at[m, k], at_x((t + k) % 4)))

    def back(m):
        for k in (1, 3, 2):
            blk = hb.at[m, (t + 4 - k) % 4]
            rdma(blk, blk, h_s.at[m, k], h_r.at[m, k], at_x((t + k) % 4)).wait_recv()
        h = hb[m].reshape(128, 1024)
        for a, lo, hi in ((0, 640, 1024), (1, 0, 640)):
            os_[m, a] = nn(h[:, lo:hi], w[lo:hi]).astype(BF).reshape(8, 16, 896)
            for i in range(8 if m else 0):
                to = cl if i == 7 else klass(OFFS[i])
                go(
                    rdma(
                        os_.at[m, a, to], ro.at[m, a, to],
                        o_s.at[m, a, i], o_r.at[m, a, i], at_y(chunks[m]),
                    )
                )

    half(0)
    fw = []
    for src, i, to_right, to_left in yc:
        to_right.wait_recv()
        blk = xd.at[left, 0, src]
        fw.append(go(rdma(blk, blk, v_s.at[0, i], v_r.at[0, i], at_y(right))))
        to_left.wait_recv()
        blk = xd.at[right, 1, src]
        fw.append(go(rdma(blk, blk, v_s.at[1, i], v_r.at[1, i], at_y(left))))
    half(1)
    half(2)
    middle(0)
    for q in fw:
        q.wait_recv()
    half(3)
    middle(1)
    middle(2)
    back(0)
    back(1)
    back(2)
    middle(3)
    back(3)

    order = [xd[chunks[m], 0].reshape(128, 896) for m in range(4)]
    xs = jnp.concatenate(order, axis=0)
    ds = jnp.concatenate([xd[chunks[m], 1].reshape(128, 896) for m in range(4)], axis=0)
    hs = hb[...].reshape(512, 1024)
    for at, n, r in ((0, 256, xs), (256, 256, xs), (512, 128, xs), (640, 384, ds)):
        gr[at : at + n] = tn(hs[:, at : at + n], r).astype(BF)
    gg_ref[0], gu_ref[0], gd_ref[0] = gr[0:304], gr[304:608], gr[640:944]

    def gather(a):
        got = []
        for i in range(8):
            k = 0 if i == 7 else OFFS[i]
            to = klass(k)
            acc = os_[0, a, to].astype(F32)
            for m in (1, 2, 3):
                ref = ro.at[m, a, to]
                rdma(
                    ref, ref, o_s.at[m, a, i], o_r.at[m, a, i], at_y(chunks[m])
                ).wait_recv()
                acc = acc + ro[m, a, to].astype(F32)
            if i == 7:
                rb[a, cl] = acc.astype(BF)
            else:
                sb[a, to] = acc.astype(BF)
                dest = at_z(-4 if i == 0 and a else k)
                got.append(
                    go(rdma(sb.at[a, to], rb.at[a, cl], c_s.at[a, i], c_r.at[a, i], dest))
                )
        return got

    def combine(a, got):
        for q in got:
            q.wait_recv()
        r = rb[a].reshape(128, 896)
        tot = sum(nn(m.T.astype(BF), r) for m in ([one] if a else weights))
        tot = tot.reshape(4, 2, 2, 8, 896)
        sides = (tot[:, 0, 0], tot[:, 1, 0])
        mine = jnp.where(c == 0, sides[0], sides[1])
        other = jnp.where(c == 0, sides[1], sides[0])
        ts[a] = other.reshape(32, 896).astype(BF)
        go(rdma(ts.at[a], rs.at[a], t_s.at[a], t_r.at[a], sib)).wait_recv()
        mine = mine + rs[a].reshape(4, 8, 896).astype(F32)
        tail = jnp.concatenate([mine[:, :, 512:896], jnp.zeros((4, 8, 128), F32)], axis=2)
        fs[a] = jnp.concatenate([mine[:, :, 0:512], tail], axis=1)
        fg[a, 0] = fs[a, zo].astype(BF)
        fg[a, 1, :, 256:512] = fs[a, zr, :, 256:512].astype(BF)
        fg[a, 2, :, 0:256] = fs[a, zl, :, 0:256].astype(BF)
        lo, hi = pl.ds(0, 256), pl.ds(256, 256)

        def hop(src, dst, i, to):
            return go(rdma(src, dst, f_s.at[a, i], f_r.at[a, i], to))

        return [
            hop(fg.at[a, 0, :, lo], f1.at[a, 0], 0, up),
            hop(fg.at[a, 0, :, hi], f1.at[a, 1], 1, down),
            hop(fg.at[a, 1, :, hi], f2.at[a, 0, :, hi], 2, up),
            hop(fg.at[a, 2, :, lo], f2.at[a, 1, :, lo], 3, down),
        ]

    def relay(a, hops):
        lo, hi = pl.ds(0, 256), pl.ds(256, 256)
        hops[0].wait_recv()
        fg[a, 1, :, 0:256] = (fs[a, zr, :, 0:256] + f1[a, 0].astype(F32)).astype(BF)
        q = rdma(fg.at[a, 1, :, lo], f2.at[a, 0, :, lo], f_s.at[a, 4], f_r.at[a, 4], up)
        hops.append(go(q))
        hops[1].wait_recv()
        fg[a, 2, :, 256:512] = (fs[a, zl, :, 256:512] + f1[a, 1].astype(F32)).astype(BF)
        q = rdma(fg.at[a, 2, :, hi], f2.at[a, 1, :, hi], f_s.at[a, 5], f_r.at[a, 5], down)
        hops.append(go(q))

    def finish(a, hops, ref):
        for q in hops[2:]:
            q.wait_recv()
        fin = fs[a, zh] + f2[a, 0].astype(F32) + f2[a, 1].astype(F32)
        ref[:, 0:512] = fin[0:8].astype(BF)
        ref[:, 512:896] = fin[8:16, 0:384].astype(BF)

    hops0 = combine(0, gather(0))
    got = gather(1)
    relay(0, hops0)
    hops1 = combine(1, got)
    relay(1, hops1)
    finish(0, hops0, mixed_ref)
    finish(1, hops1, gtok_ref)

    for q in pend:
        q.wait_send()


def shards(tokens, out_grad, expert_ids, gate_probs, w_gate, w_up, w_down):
    vm = pl.BlockSpec(memory_space=pltpu.VMEM)
    hbm = pl.BlockSpec(memory_space=pltpu.HBM)
    dma = pltpu.SemaphoreType.DMA
    mixed, gtok, gg, gu, gd = pl.pallas_call(
        kernel,
        out_shape=(
            jax.ShapeDtypeStruct((8, 896), BF),
            jax.ShapeDtypeStruct((8, 896), BF),
            jax.ShapeDtypeStruct((1, 304, 896), BF),
            jax.ShapeDtypeStruct((1, 304, 896), BF),
            jax.ShapeDtypeStruct((1, 304, 896), BF),
        ),
        in_specs=[vm] * 4 + [hbm] * 3,
        out_specs=(vm,) * 5,
        scratch_shapes=[
            pltpu.VMEM((1024, 896), BF),
            pltpu.VMEM((4, 2, 16, 1024), BF),
            pltpu.VMEM((2, 8, 16, 896), BF),
            pltpu.VMEM((4, 2, 8, 16, 896), BF),
            pltpu.VMEM((4, 4, 32, 1024), BF),
            pltpu.VMEM((4, 4, 32, 1024), BF),
            pltpu.VMEM((4, 4, 32, 1024), BF),
            pltpu.VMEM((4, 2, 8, 16, 896), BF),
            pltpu.VMEM((4, 2, 8, 16, 896), BF),
            pltpu.VMEM((2, 8, 16, 896), BF),
            pltpu.VMEM((2, 8, 16, 896), BF),
            pltpu.VMEM((2, 32, 896), BF),
            pltpu.VMEM((2, 32, 896), BF),
            pltpu.VMEM((2, 4, 16, 512), F32),
            pltpu.VMEM((2, 2, 16, 256), BF),
            pltpu.VMEM((2, 3, 16, 512), BF),
            pltpu.VMEM((2, 2, 16, 512), BF),
            pltpu.VMEM((1024, 896), BF),
        ]
        + [dma((6,))] * 2
        + [dma((4,))] * 2
        + [dma((8,))] * 2
        + [dma((2, 8))] * 4
        + [dma((4, 4))] * 4
        + [dma((4, 2, 8))] * 2
        + [dma((2, 7))] * 2
        + [dma((2,))] * 2
        + [dma((2, 6))] * 2
        + [dma((3,))],
        compiler_params=pltpu.CompilerParams(
            collective_id=0, has_side_effects=True, vmem_limit_bytes=60 << 20
        ),
        cost_estimate=pl.CostEstimate(
            flops=2600000000, bytes_accessed=4000000, transcendentals=40000
        ),
    )(
        tokens, out_grad, expert_ids.T, gate_probs.T,
        w_gate.transpose(0, 2, 1), w_up.transpose(0, 2, 1), w_down,
    )
    return mixed, gtok, gg.transpose(0, 2, 1), gu.transpose(0, 2, 1), gd


def solution(mesh):
    wide = P(("dp", "expert"), "tp")
    rows = P(("dp", "expert"), None)
    up = P("expert", "tp", "dp")
    down = P("expert", "dp", "tp")
    return jax.shard_map(
        shards,
        mesh=mesh,
        in_specs=(wide, wide, rows, rows, up, up, down),
        out_specs=(wide, wide, up, up, down),
        check_vma=False,
    )
```

```python
import jax
import jax.numpy as jnp
from jax import lax
from jax.experimental import pallas as pl
from jax.experimental.pallas import tpu as pltpu
from jax.sharding import PartitionSpec as P

MESH = pl.DeviceIdType.MESH
BF = jnp.bfloat16
F32 = jnp.float32


def nn(a, b):
    return lax.dot_general(a, b, (((1,), (0,)), ((), ())), preferred_element_type=F32)


def nt(a, b):
    return lax.dot_general(a, b, (((1,), (1,)), ((), ())), preferred_element_type=F32)


def tn(a, b):
    return lax.dot_general(a, b, (((0,), (0,)), ((), ())), preferred_element_type=F32)


OFFS = (4, 3, -3, 2, -2, 1, -1)


def routing(ids, probs, zh, c):
    rank = jnp.zeros((2, 8), jnp.int32)
    for d in range(1, 8):
        before = jnp.concatenate([jnp.full((2, d), -1, jnp.int32), ids[:, : 8 - d]], axis=1)
        same = (ids == before[0:1]) | (ids == before[1:2])
        rank = rank + jnp.where(same, 1, 0)
    slot = (ids >> 1) * 16 + (ids & 1) * 128 + rank + (zh * 4 + c * 2 + 1)
    slot = slot.astype(F32)
    hi = probs.astype(BF).astype(F32)
    mid = (probs - hi).astype(BF).astype(F32)
    low = probs - hi - mid
    table = [slot] + [part[i : i + 1] for i in range(2) for part in (hi, mid, low)]
    table = jnp.concatenate(table, axis=0)
    table = jnp.concatenate([table] * 16, axis=1)
    here = (lax.broadcasted_iota(jnp.int32, (8, 128), 1) // 16) == (zh * 2 + c)
    table = jnp.where(here, table, 0.0)
    return jnp.concatenate([table, jnp.zeros((8, 128), F32)], axis=0).astype(BF)


def kernel(
    tok_ref, og_ref, ids_ref, probs_ref, wg_ref, wu_ref, wd_ref,
    fin_ref, gr,
    w, zed, sx, xd, ps, rp, hb, os_, ro, sb, rb, ts, rs, fs, f1, fg, f2,
    a_s, a_r, s_s, s_r, b_s, b_r, y_s, y_r, v_s, v_r, p_s, p_r, h_s, h_r,
    o_s, o_r, c_s, c_r, t_s, t_r, f_s, f_r, w_m,
):
    dp = lax.axis_index("dp")
    ex = lax.axis_index("expert")
    t = lax.axis_index("tp")
    zh, y, cl, c = dp // 4, dp % 4, ex // 2, ex % 2
    z = zh * 8 + cl
    sc = 1 - c

    def at_z(k):
        zz = (z + k + 32) % 32
        return ((zz // 8) * 4 + y, (zz % 8) * 2 + c, t)

    def at_y(yy):
        return (zh * 4 + yy, ex, t)

    def at_x(tt):
        return (dp, ex, tt)

    def klass(k):
        return (cl + k + 8) % 8

    sib = (dp, cl * 2 + sc, t)

    def rdma(src, dst, ss, rr, to):
        return pltpu.make_async_remote_copy(
            src, dst, ss, rr, device_id=to, device_id_type=MESH
        )

    peers = [at_z(k) for k in (8, -8, 4, -4, 3, -3, 2, -2, 1, -1)]
    peers += [at_y((y + k) % 4) for k in (1, 2, 3)]
    peers += [at_x((t + k) % 4) for k in (1, 2, 3)]
    peers += [sib]
    bar = pltpu.get_barrier_semaphore()
    for p in peers:
        pl.semaphore_signal(bar, inc=1, device_id=p, device_id_type=MESH)

    zed[zh, c, :, 0:896] = jnp.concatenate([tok_ref[...], og_ref[...]], axis=0)
    zed[zh, c, :, 896:1024] = routing(ids_ref[...], probs_ref[...], zh, c)
    loads = []
    for i, (ref, at) in enumerate(((wg_ref, 0), (wu_ref, 304), (wd_ref, 640))):
        q = pltpu.make_async_copy(ref.at[0], w.at[pl.ds(at, 304)], w_m.at[i])
        q.start()
        loads.append(q)
    w[608:640] = jnp.zeros((32, 896), BF)
    w[944:1024] = jnp.zeros((80, 896), BF)
    pl.semaphore_wait(bar, len(peers))

    pend = []

    def go(copy):
        copy.start()
        pend.append(copy)
        return copy

    up, down = at_z(8), at_z(-8)
    zr, zl, zo = (zh + 1) % 4, (zh + 3) % 4, (zh + 2) % 4
    halves = (pl.ds(0, 512), pl.ds(512, 512))

    def along(who, h, i, to):
        blk = zed.at[who, c, :, halves[h]]
        return go(rdma(blk, blk, a_s.at[i], a_r.at[i], to))

    ac = [along(zh, i // 2 ^ i % 2, i, (up, down)[i % 2]) for i in range(4)]
    sc_copies = []

    def across(who):
        blk = zed.at[who, c]
        i = len(sc_copies)
        sc_copies.append(go(rdma(blk, blk, s_s.at[i], s_r.at[i], sib)))

    across(zh)
    ac[0].wait_recv()
    ac.append(along(zl, 0, 4, up))
    ac[1].wait_recv()
    ac.append(along(zr, 1, 5, down))
    ac[2].wait_recv()
    across(zl)
    ac[3].wait_recv()
    across(zr)
    ac[4].wait_recv()
    ac[5].wait_recv()
    across(zo)
    for q in sc_copies:
        q.wait_recv()

    meta = jnp.zeros((16, 128), F32)
    for j in range(4):
        for cc in range(2):
            meta = meta + zed[j, cc, :, 896:1024].astype(F32)
    rid = (lax.broadcasted_iota(jnp.int32, (128, 128), 0) + 1 + 128 * c).astype(F32)
    first = rid == meta[0:1, :]
    second = rid == meta[1:2, :]
    one = jnp.where(first | second, 1.0, 0.0)
    weights = [
        jnp.where(first, meta[2 + i : 3 + i, :], 0.0)
        + jnp.where(second, meta[5 + i : 6 + i, :], 0.0)
        for i in range(3)
    ]
    is_tok = (lax.broadcasted_iota(jnp.int32, (128, 128), 1) % 16) < 8
    rows = zed[:, :, :, 0:896].reshape(128, 896)
    x_slots = nn(jnp.where(is_tok, one, 0.0).astype(BF), rows).astype(BF)
    dy_slots = sum(nn(jnp.where(is_tok, 0.0, m).astype(BF), rows) for m in weights)
    dy_slots = dy_slots.astype(BF)
    sx[0] = x_slots.reshape(8, 16, 896)
    sx[1] = dy_slots.reshape(8, 16, 896)

    def near(src, dst, ss, rr, i):
        k = OFFS[i]
        to = klass(k)
        if i:
            return [go(rdma(src.at[:, to], dst(slice(None)), ss.at[i], rr.at[i], at_z(k)))]
        return [
            go(rdma(src.at[0, to], dst(0), ss.at[0], rr.at[0], at_z(4))),
            go(rdma(src.at[1, to], dst(1), ss.at[7], rr.at[7], at_z(-4))),
        ]

    got = {i: near(sx, lambda a: xd.at[y, a, cl], b_s, b_r, i) for i in range(7)}
    xd[y, :, cl] = sx[:, cl]

    left, right = (y + 3) % 4, (y + 1) % 4
    yc = []
    for i in (7, 5, 6, 3, 4, 1, 2, 0):
        src = cl if i == 7 else klass(-OFFS[i])
        if i < 7:
            for q in got[i]:
                q.wait_recv()
        blk = xd.at[y, :, src]
        yc.append(
            (
                src,
                i,
                go(rdma(blk, blk, y_s.at[0, i], y_r.at[0, i], at_y(right))),
                go(rdma(blk, blk, y_s.at[1, i], y_r.at[1, i], at_y(left))),
            )
        )
    for q in loads:
        q.wait()

    chunks = (y, left, right, (y + 2) % 4)

    def half(m):
        yy = chunks[m]
        gu = nt(xd[yy, 0].reshape(128, 896), w[0:640])
        b = nt(xd[yy, 1].reshape(128, 896), w[640:1024])
        ps[m, :, :, 0:640] = gu.astype(BF).reshape(4, 32, 640)
        ps[m, :, :, 640:1024] = b.astype(BF).reshape(4, 32, 384)
        for k in (2, 1, 3):
            q = (t + k) % 4
            go(rdma(ps.at[m, q], rp.at[m, k], p_s.at[m, k], p_r.at[m, k], at_x(q)))

    def middle(m):
        acc = ps[m, t].astype(F32)
        for k in (1, 3, 2):
            ref = rp.at[m, k]
            rdma(ref, ref, p_s.at[m, k], p_r.at[m, k], at_x((t + k) % 4)).wait_recv()
            acc = acc + rp[m, k].astype(F32)
        g, u, b = acc[:, 0:304], acc[:, 304:608], acc[:, 640:944]
        s = jax.nn.sigmoid(g)
        sw = g * s
        hb[m, t] = jnp.concatenate(
            [
                b * u * (s * (1.0 + g * (1.0 - s))),
                b * sw,
                jnp.zeros((32, 32), F32),
                sw * u,
                jnp.zeros((32, 80), F32),
            ],
            axis=1,
        ).astype(BF)
        for k in (2, 1, 3):
            blk = hb.at[m, t]
            go(rdma(blk, blk, h_s.at[m, k], h_r.at[m, k], at_x((t + k) % 4)))

    def back(m):
        for k in (1, 3, 2):
            blk = hb.at[m, (t + 4 - k) % 4]
            rdma(blk, blk, h_s.at[m, k], h_r.at[m, k], at_x((t + k) % 4)).wait_recv()
        h = hb[m].reshape(128, 1024)
        for a, lo, hi in ((0, 640, 1024), (1, 0, 640)):
            os_[m, a] = nn(h[:, lo:hi], w[lo:hi]).astype(BF).reshape(8, 16, 896)
            for i in range(8 if m else 0):
                to = cl if i == 7 else klass(OFFS[i])
                go(
                    rdma(
                        os_.at[m, a, to], ro.at[m, a, to],
                        o_s.at[m, a, i], o_r.at[m, a, i], at_y(chunks[m]),
                    )
                )

    half(0)
    fw = []
    for src, i, to_right, to_left in yc:
        to_right.wait_recv()
        blk = xd.at[left, 0, src]
        fw.append(go(rdma(blk, blk, v_s.at[0, i], v_r.at[0, i], at_y(right))))
        to_left.wait_recv()
        blk = xd.at[right, 1, src]
        fw.append(go(rdma(blk, blk, v_s.at[1, i], v_r.at[1, i], at_y(left))))
    half(1)
    half(2)
    middle(0)
    middle(1)
    middle(2)
    back(1)
    back(2)
    for q in fw:
        q.wait_recv()
    half(3)
    middle(3)
    back(3)
    back(0)

    order = [xd[chunks[m], 0].reshape(128, 896) for m in range(4)]
    xs = jnp.concatenate(order, axis=0)
    ds = jnp.concatenate([xd[chunks[m], 1].reshape(128, 896) for m in range(4)], axis=0)
    hs = hb[...].reshape(512, 1024)
    for at, n, r in ((0, 256, xs), (256, 256, xs), (512, 128, xs), (640, 384, ds)):
        gr[at : at + n] = tn(hs[:, at : at + n], r).astype(BF)
    def gather(a):
        got = []
        for i in range(8):
            k = 0 if i == 7 else OFFS[i]
            to = klass(k)
            acc = os_[0, a, to].astype(F32)
            for m in (1, 2, 3):
                ref = ro.at[m, a, to]
                rdma(
                    ref, ref, o_s.at[m, a, i], o_r.at[m, a, i], at_y(chunks[m])
                ).wait_recv()
                acc = acc + ro[m, a, to].astype(F32)
            if i == 7:
                rb[a, cl] = acc.astype(BF)
            else:
                sb[a, to] = acc.astype(BF)
                dest = at_z(-4 if i == 0 and a else k)
                got.append(
                    go(rdma(sb.at[a, to], rb.at[a, cl], c_s.at[a, i], c_r.at[a, i], dest))
                )
        return got

    def combine(a, got):
        for q in got:
            q.wait_recv()
        r = rb[a].reshape(128, 896)
        tot = sum(nn(m.T.astype(BF), r) for m in ([one] if a else weights))
        tot = tot.reshape(4, 2, 2, 8, 896)
        sides = (tot[:, 0, 0], tot[:, 1, 0])
        mine = jnp.where(c == 0, sides[0], sides[1])
        other = jnp.where(c == 0, sides[1], sides[0])
        ts[a] = other.reshape(32, 896).astype(BF)
        go(rdma(ts.at[a], rs.at[a], t_s.at[a], t_r.at[a], sib)).wait_recv()
        mine = mine + rs[a].reshape(4, 8, 896).astype(F32)
        tail = jnp.concatenate([mine[:, :, 512:896], jnp.zeros((4, 8, 128), F32)], axis=2)
        fs[a] = jnp.concatenate([mine[:, :, 0:512], tail], axis=1)
        fg[a, 0] = fs[a, zo].astype(BF)
        fg[a, 1, :, 256:512] = fs[a, zr, :, 256:512].astype(BF)
        fg[a, 2, :, 0:256] = fs[a, zl, :, 0:256].astype(BF)
        lo, hi = pl.ds(0, 256), pl.ds(256, 256)

        def hop(src, dst, i, to):
            return go(rdma(src, dst, f_s.at[a, i], f_r.at[a, i], to))

        return [
            hop(fg.at[a, 0, :, lo], f1.at[a, 0], 0, up),
            hop(fg.at[a, 0, :, hi], f1.at[a, 1], 1, down),
            hop(fg.at[a, 1, :, hi], f2.at[a, 0, :, hi], 2, up),
            hop(fg.at[a, 2, :, lo], f2.at[a, 1, :, lo], 3, down),
        ]

    def relay(a, hops):
        lo, hi = pl.ds(0, 256), pl.ds(256, 256)
        hops[0].wait_recv()
        fg[a, 1, :, 0:256] = (fs[a, zr, :, 0:256] + f1[a, 0].astype(F32)).astype(BF)
        q = rdma(fg.at[a, 1, :, lo], f2.at[a, 0, :, lo], f_s.at[a, 4], f_r.at[a, 4], up)
        hops.append(go(q))
        hops[1].wait_recv()
        fg[a, 2, :, 256:512] = (fs[a, zl, :, 256:512] + f1[a, 1].astype(F32)).astype(BF)
        q = rdma(fg.at[a, 2, :, hi], f2.at[a, 1, :, hi], f_s.at[a, 5], f_r.at[a, 5], down)
        hops.append(go(q))

    def finish(a, hops):
        for q in hops[2:]:
            q.wait_recv()
        fin = fs[a, zh] + f2[a, 0].astype(F32) + f2[a, 1].astype(F32)
        fin_ref[a, :, 0:512] = fin[0:8].astype(BF)
        fin_ref[a, :, 512:896] = fin[8:16, 0:384].astype(BF)

    hops0 = combine(0, gather(0))
    got = gather(1)
    relay(0, hops0)
    hops1 = combine(1, got)
    relay(1, hops1)
    finish(0, hops0)
    finish(1, hops1)

    for q in pend:
        q.wait_send()


def unstack(fin_ref, gr_ref, mixed_ref, gtok_ref, gg_ref, gu_ref, gd_ref, sems):
    pairs = [(fin_ref.at[0], mixed_ref), (fin_ref.at[1], gtok_ref)]
    for at, ref in ((0, gg_ref), (304, gu_ref), (640, gd_ref)):
        pairs.append((gr_ref.at[pl.ds(at, 304)], ref.at[0]))
    copies = [pltpu.make_async_copy(p, q, sems.at[i]) for i, (p, q) in enumerate(pairs)]
    for q in copies:
        q.start()
    for q in copies:
        q.wait()


def shards(tokens, out_grad, expert_ids, gate_probs, w_gate, w_up, w_down):
    vm = pl.BlockSpec(memory_space=pltpu.VMEM)
    hbm = pl.BlockSpec(memory_space=pltpu.HBM)
    dma = pltpu.SemaphoreType.DMA
    fin, grads = pl.pallas_call(
        kernel,
        out_shape=(
            jax.ShapeDtypeStruct((2, 8, 896), BF),
            jax.ShapeDtypeStruct((1024, 896), BF),
        ),
        in_specs=[vm] * 4 + [hbm] * 3,
        out_specs=(vm,) * 2,
        scratch_shapes=[
            pltpu.VMEM((1024, 896), BF),
            pltpu.VMEM((4, 2, 16, 1024), BF),
            pltpu.VMEM((2, 8, 16, 896), BF),
            pltpu.VMEM((4, 2, 8, 16, 896), BF),
            pltpu.VMEM((4, 4, 32, 1024), BF),
            pltpu.VMEM((4, 4, 32, 1024), BF),
            pltpu.VMEM((4, 4, 32, 1024), BF),
            pltpu.VMEM((4, 2, 8, 16, 896), BF),
            pltpu.VMEM((4, 2, 8, 16, 896), BF),
            pltpu.VMEM((2, 8, 16, 896), BF),
            pltpu.VMEM((2, 8, 16, 896), BF),
            pltpu.VMEM((2, 32, 896), BF),
            pltpu.VMEM((2, 32, 896), BF),
            pltpu.VMEM((2, 4, 16, 512), F32),
            pltpu.VMEM((2, 2, 16, 256), BF),
            pltpu.VMEM((2, 3, 16, 512), BF),
            pltpu.VMEM((2, 2, 16, 512), BF),
        ]
        + [dma((6,))] * 2
        + [dma((4,))] * 2
        + [dma((8,))] * 2
        + [dma((2, 8))] * 4
        + [dma((4, 4))] * 4
        + [dma((4, 2, 8))] * 2
        + [dma((2, 7))] * 2
        + [dma((2,))] * 2
        + [dma((2, 6))] * 2
        + [dma((3,))],
        compiler_params=pltpu.CompilerParams(
            collective_id=0, has_side_effects=True, vmem_limit_bytes=60 << 20
        ),
        cost_estimate=pl.CostEstimate(
            flops=2600000000, bytes_accessed=4000000, transcendentals=40000
        ),
    )(
        tokens, out_grad, expert_ids.T, gate_probs.T,
        w_gate.transpose(0, 2, 1), w_up.transpose(0, 2, 1), w_down,
    )
    mixed, gtok, gg, gu, gd = pl.pallas_call(
        unstack,
        out_shape=(
            jax.ShapeDtypeStruct((8, 896), BF),
            jax.ShapeDtypeStruct((8, 896), BF),
            jax.ShapeDtypeStruct((1, 304, 896), BF),
            jax.ShapeDtypeStruct((1, 304, 896), BF),
            jax.ShapeDtypeStruct((1, 304, 896), BF),
        ),
        in_specs=[vm] * 2,
        out_specs=(hbm,) * 5,
        scratch_shapes=[dma((5,))],
        compiler_params=pltpu.CompilerParams(vmem_limit_bytes=60 << 20),
    )(fin, grads)
    return mixed, gtok, gg.transpose(0, 2, 1), gu.transpose(0, 2, 1), gd


def solution(mesh):
    wide = P(("dp", "expert"), "tp")
    rows = P(("dp", "expert"), None)
    up = P("expert", "tp", "dp")
    down = P("expert", "dp", "tp")
    return jax.shard_map(
        shards,
        mesh=mesh,
        in_specs=(wide, wide, rows, rows, up, up, down),
        out_specs=(wide, wide, up, up, down),
        check_vma=False,
    )
```

```python
import jax
import jax.numpy as jnp
from jax import lax
from jax.experimental import pallas as pl
from jax.experimental.pallas import tpu as pltpu
from jax.sharding import PartitionSpec as P

MESH = pl.DeviceIdType.MESH
BF = jnp.bfloat16
F32 = jnp.float32


def nn(a, b):
    return lax.dot_general(a, b, (((1,), (0,)), ((), ())), preferred_element_type=F32)


def nt(a, b):
    return lax.dot_general(a, b, (((1,), (1,)), ((), ())), preferred_element_type=F32)


def tn(a, b):
    return lax.dot_general(a, b, (((0,), (0,)), ((), ())), preferred_element_type=F32)


OFFS = (4, 3, -3, 2, -2, 1, -1)


def routing(ids, probs, zh, c):
    rank = jnp.zeros((2, 8), jnp.int32)
    for d in range(1, 8):
        before = jnp.concatenate([jnp.full((2, d), -1, jnp.int32), ids[:, : 8 - d]], axis=1)
        same = (ids == before[0:1]) | (ids == before[1:2])
        rank = rank + jnp.where(same, 1, 0)
    slot = (ids >> 1) * 16 + (ids & 1) * 128 + rank + (zh * 4 + c * 2 + 1)
    slot = slot.astype(F32)
    hi = probs.astype(BF).astype(F32)
    mid = (probs - hi).astype(BF).astype(F32)
    low = probs - hi - mid
    table = [slot] + [part[i : i + 1] for i in range(2) for part in (hi, mid, low)]
    table = jnp.concatenate(table, axis=0)
    table = jnp.concatenate([table] * 16, axis=1)
    here = (lax.broadcasted_iota(jnp.int32, (8, 128), 1) // 16) == (zh * 2 + c)
    table = jnp.where(here, table, 0.0)
    return jnp.concatenate([table, jnp.zeros((8, 128), F32)], axis=0).astype(BF)


def kernel(
    tok_ref, og_ref, ids_ref, probs_ref, wg_ref, wu_ref, wd_ref,
    fin_ref, grads_ref,
    w, zed, sx, xd, ps, rp, hb, os_, ro, sb, rb, ts, rs, fs, f1, fg, f2, gr,
    a_s, a_r, s_s, s_r, b_s, b_r, y_s, y_r, v_s, v_r, p_s, p_r, h_s, h_r,
    o_s, o_r, c_s, c_r, t_s, t_r, f_s, f_r, w_m, g_m,
):
    dp = lax.axis_index("dp")
    ex = lax.axis_index("expert")
    t = lax.axis_index("tp")
    zh, y, cl, c = dp // 4, dp % 4, ex // 2, ex % 2
    z = zh * 8 + cl
    sc = 1 - c

    def at_z(k):
        zz = (z + k + 32) % 32
        return ((zz // 8) * 4 + y, (zz % 8) * 2 + c, t)

    def at_y(yy):
        return (zh * 4 + yy, ex, t)

    def at_x(tt):
        return (dp, ex, tt)

    def klass(k):
        return (cl + k + 8) % 8

    sib = (dp, cl * 2 + sc, t)

    def rdma(src, dst, ss, rr, to):
        return pltpu.make_async_remote_copy(
            src, dst, ss, rr, device_id=to, device_id_type=MESH
        )

    peers = [at_z(k) for k in (8, -8, 4, -4, 3, -3, 2, -2, 1, -1)]
    peers += [at_y((y + k) % 4) for k in (1, 2, 3)]
    peers += [at_x((t + k) % 4) for k in (1, 2, 3)]
    peers += [sib]
    bar = pltpu.get_barrier_semaphore()
    for p in peers:
        pl.semaphore_signal(bar, inc=1, device_id=p, device_id_type=MESH)

    zed[zh, c, :, 0:896] = jnp.concatenate([tok_ref[...], og_ref[...]], axis=0)
    zed[zh, c, :, 896:1024] = routing(ids_ref[...], probs_ref[...], zh, c)
    loads = []
    for i, (ref, at) in enumerate(((wg_ref, 0), (wu_ref, 304), (wd_ref, 640))):
        q = pltpu.make_async_copy(ref.at[0], w.at[pl.ds(at, 304)], w_m.at[i])
        q.start()
        loads.append(q)
    w[608:640] = jnp.zeros((32, 896), BF)
    w[944:1024] = jnp.zeros((80, 896), BF)
    pl.semaphore_wait(bar, len(peers))

    pend = []

    def go(copy):
        copy.start()
        pend.append(copy)
        return copy

    up, down = at_z(8), at_z(-8)
    zr, zl, zo = (zh + 1) % 4, (zh + 3) % 4, (zh + 2) % 4
    halves = (pl.ds(0, 512), pl.ds(512, 512))

    def along(who, h, i, to):
        blk = zed.at[who, c, :, halves[h]]
        return go(rdma(blk, blk, a_s.at[i], a_r.at[i], to))

    ac = [along(zh, i // 2 ^ i % 2, i, (up, down)[i % 2]) for i in range(4)]
    sc_copies = []

    def across(who):
        blk = zed.at[who, c]
        i = len(sc_copies)
        sc_copies.append(go(rdma(blk, blk, s_s.at[i], s_r.at[i], sib)))

    across(zh)
    ac[0].wait_recv()
    ac.append(along(zl, 0, 4, up))
    ac[1].wait_recv()
    ac.append(along(zr, 1, 5, down))
    ac[2].wait_recv()
    across(zl)
    ac[3].wait_recv()
    across(zr)
    ac[4].wait_recv()
    ac[5].wait_recv()
    across(zo)
    for q in sc_copies:
        q.wait_recv()

    meta = jnp.zeros((16, 128), F32)
    for j in range(4):
        for cc in range(2):
            meta = meta + zed[j, cc, :, 896:1024].astype(F32)
    rid = (lax.broadcasted_iota(jnp.int32, (128, 128), 0) + 1 + 128 * c).astype(F32)
    first = rid == meta[0:1, :]
    second = rid == meta[1:2, :]
    one = jnp.where(first | second, 1.0, 0.0)
    weights = [
        jnp.where(first, meta[2 + i : 3 + i, :], 0.0)
        + jnp.where(second, meta[5 + i : 6 + i, :], 0.0)
        for i in range(3)
    ]
    is_tok = (lax.broadcasted_iota(jnp.int32, (128, 128), 1) % 16) < 8
    rows = zed[:, :, :, 0:896].reshape(128, 896)
    x_slots = nn(jnp.where(is_tok, one, 0.0).astype(BF), rows).astype(BF)
    dy_slots = sum(nn(jnp.where(is_tok, 0.0, m).astype(BF), rows) for m in weights)
    dy_slots = dy_slots.astype(BF)
    sx[0] = x_slots.reshape(8, 16, 896)
    sx[1] = dy_slots.reshape(8, 16, 896)

    def near(src, dst, ss, rr, i):
        k = OFFS[i]
        to = klass(k)
        if i:
            return [go(rdma(src.at[:, to], dst(slice(None)), ss.at[i], rr.at[i], at_z(k)))]
        return [
            go(rdma(src.at[0, to], dst(0), ss.at[0], rr.at[0], at_z(4))),
            go(rdma(src.at[1, to], dst(1), ss.at[7], rr.at[7], at_z(-4))),
        ]

    got = {i: near(sx, lambda a: xd.at[y, a, cl], b_s, b_r, i) for i in range(7)}
    xd[y, :, cl] = sx[:, cl]

    left, right = (y + 3) % 4, (y + 1) % 4
    yc = []
    for i in (7, 5, 6, 3, 4, 1, 2, 0):
        src = cl if i == 7 else klass(-OFFS[i])
        if i < 7:
            for q in got[i]:
                q.wait_recv()
        blk = xd.at[y, :, src]
        yc.append(
            (
                src,
                i,
                go(rdma(blk, blk, y_s.at[0, i], y_r.at[0, i], at_y(right))),
                go(rdma(blk, blk, y_s.at[1, i], y_r.at[1, i], at_y(left))),
            )
        )
    for q in loads:
        q.wait()

    chunks = (y, left, right, (y + 2) % 4)

    def half(m):
        yy = chunks[m]
        gu = nt(xd[yy, 0].reshape(128, 896), w[0:640])
        b = nt(xd[yy, 1].reshape(128, 896), w[640:1024])
        ps[m, :, :, 0:640] = gu.astype(BF).reshape(4, 32, 640)
        ps[m, :, :, 640:1024] = b.astype(BF).reshape(4, 32, 384)
        for k in (2, 1, 3):
            q = (t + k) % 4
            go(rdma(ps.at[m, q], rp.at[m, k], p_s.at[m, k], p_r.at[m, k], at_x(q)))

    def middle(m):
        acc = ps[m, t].astype(F32)
        for k in (1, 3, 2):
            ref = rp.at[m, k]
            rdma(ref, ref, p_s.at[m, k], p_r.at[m, k], at_x((t + k) % 4)).wait_recv()
            acc = acc + rp[m, k].astype(F32)
        g, u, b = acc[:, 0:304], acc[:, 304:608], acc[:, 640:944]
        s = jax.nn.sigmoid(g)
        sw = g * s
        hb[m, t] = jnp.concatenate(
            [
                b * u * (s * (1.0 + g * (1.0 - s))),
                b * sw,
                jnp.zeros((32, 32), F32),
                sw * u,
                jnp.zeros((32, 80), F32),
            ],
            axis=1,
        ).astype(BF)
        for k in (2, 1, 3):
            blk = hb.at[m, t]
            go(rdma(blk, blk, h_s.at[m, k], h_r.at[m, k], at_x((t + k) % 4)))

    def back(m):
        for k in (1, 3, 2):
            blk = hb.at[m, (t + 4 - k) % 4]
            rdma(blk, blk, h_s.at[m, k], h_r.at[m, k], at_x((t + k) % 4)).wait_recv()
        h = hb[m].reshape(128, 1024)
        for a, lo, hi in ((0, 640, 1024), (1, 0, 640)):
            os_[m, a] = nn(h[:, lo:hi], w[lo:hi]).astype(BF).reshape(8, 16, 896)
            for i in range(8 if m else 0):
                to = cl if i == 7 else klass(OFFS[i])
                go(
                    rdma(
                        os_.at[m, a, to], ro.at[m, a, to],
                        o_s.at[m, a, i], o_r.at[m, a, i], at_y(chunks[m]),
                    )
                )

    half(0)
    fw = []
    for src, i, to_right, to_left in yc:
        to_right.wait_recv()
        blk = xd.at[left, 0, src]
        fw.append(go(rdma(blk, blk, v_s.at[0, i], v_r.at[0, i], at_y(right))))
        to_left.wait_recv()
        blk = xd.at[right, 1, src]
        fw.append(go(rdma(blk, blk, v_s.at[1, i], v_r.at[1, i], at_y(left))))
    half(1)
    half(2)
    middle(0)
    middle(1)
    middle(2)
    back(1)
    back(2)
    for q in fw:
        q.wait_recv()
    half(3)
    middle(3)
    back(3)
    back(0)

    order = [xd[chunks[m], 0].reshape(128, 896) for m in range(4)]
    xs = jnp.concatenate(order, axis=0)
    ds = jnp.concatenate([xd[chunks[m], 1].reshape(128, 896) for m in range(4)], axis=0)
    hs = hb[...].reshape(512, 1024)
    for at, n, r in ((0, 256, xs), (256, 256, xs), (512, 128, xs), (640, 384, ds)):
        gr[at : at + n] = tn(hs[:, at : at + n], r).astype(BF)
    save = pltpu.make_async_copy(gr, grads_ref, g_m)
    save.start()

    def gather(a):
        got = []
        for i in range(8):
            k = 0 if i == 7 else OFFS[i]
            to = klass(k)
            acc = os_[0, a, to].astype(F32)
            for m in (1, 2, 3):
                ref = ro.at[m, a, to]
                rdma(
                    ref, ref, o_s.at[m, a, i], o_r.at[m, a, i], at_y(chunks[m])
                ).wait_recv()
                acc = acc + ro[m, a, to].astype(F32)
            if i == 7:
                rb[a, cl] = acc.astype(BF)
            else:
                sb[a, to] = acc.astype(BF)
                dest = at_z(-4 if i == 0 and a else k)
                got.append(
                    go(rdma(sb.at[a, to], rb.at[a, cl], c_s.at[a, i], c_r.at[a, i], dest))
                )
        return got

    def combine(a, got):
        for q in got:
            q.wait_recv()
        r = rb[a].reshape(128, 896)
        tot = sum(nn(m.T.astype(BF), r) for m in ([one] if a else weights))
        tot = tot.reshape(4, 2, 2, 8, 896)
        sides = (tot[:, 0, 0], tot[:, 1, 0])
        mine = jnp.where(c == 0, sides[0], sides[1])
        other = jnp.where(c == 0, sides[1], sides[0])
        ts[a] = other.reshape(32, 896).astype(BF)
        go(rdma(ts.at[a], rs.at[a], t_s.at[a], t_r.at[a], sib)).wait_recv()
        mine = mine + rs[a].reshape(4, 8, 896).astype(F32)
        tail = jnp.concatenate([mine[:, :, 512:896], jnp.zeros((4, 8, 128), F32)], axis=2)
        fs[a] = jnp.concatenate([mine[:, :, 0:512], tail], axis=1)
        fg[a, 0] = fs[a, zo].astype(BF)
        fg[a, 1, :, 256:512] = fs[a, zr, :, 256:512].astype(BF)
        fg[a, 2, :, 0:256] = fs[a, zl, :, 0:256].astype(BF)
        lo, hi = pl.ds(0, 256), pl.ds(256, 256)

        def hop(src, dst, i, to):
            return go(rdma(src, dst, f_s.at[a, i], f_r.at[a, i], to))

        return [
            hop(fg.at[a, 0, :, lo], f1.at[a, 0], 0, up),
            hop(fg.at[a, 0, :, hi], f1.at[a, 1], 1, down),
            hop(fg.at[a, 1, :, hi], f2.at[a, 0, :, hi], 2, up),
            hop(fg.at[a, 2, :, lo], f2.at[a, 1, :, lo], 3, down),
        ]

    def relay(a, hops):
        lo, hi = pl.ds(0, 256), pl.ds(256, 256)
        hops[0].wait_recv()
        fg[a, 1, :, 0:256] = (fs[a, zr, :, 0:256] + f1[a, 0].astype(F32)).astype(BF)
        q = rdma(fg.at[a, 1, :, lo], f2.at[a, 0, :, lo], f_s.at[a, 4], f_r.at[a, 4], up)
        hops.append(go(q))
        hops[1].wait_recv()
        fg[a, 2, :, 256:512] = (fs[a, zl, :, 256:512] + f1[a, 1].astype(F32)).astype(BF)
        q = rdma(fg.at[a, 2, :, hi], f2.at[a, 1, :, hi], f_s.at[a, 5], f_r.at[a, 5], down)
        hops.append(go(q))

    def finish(a, hops):
        for q in hops[2:]:
            q.wait_recv()
        fin = fs[a, zh] + f2[a, 0].astype(F32) + f2[a, 1].astype(F32)
        fin_ref[a, :, 0:512] = fin[0:8].astype(BF)
        fin_ref[a, :, 512:896] = fin[8:16, 0:384].astype(BF)

    hops0 = combine(0, gather(0))
    got = gather(1)
    relay(0, hops0)
    hops1 = combine(1, got)
    relay(1, hops1)
    finish(0, hops0)
    finish(1, hops1)

    for q in pend:
        q.wait_send()
    save.wait()


def unstack(fin_ref, gr_ref, mixed_ref, gtok_ref, gg_ref, gu_ref, gd_ref, sems):
    pairs = [(fin_ref.at[0], mixed_ref), (fin_ref.at[1], gtok_ref)]
    for at, ref in ((0, gg_ref), (304, gu_ref), (640, gd_ref)):
        pairs.append((gr_ref.at[pl.ds(at, 304)], ref.at[0]))
    copies = [pltpu.make_async_copy(p, q, sems.at[i]) for i, (p, q) in enumerate(pairs)]
    for q in copies:
        q.start()
    for q in copies:
        q.wait()


def shards(tokens, out_grad, expert_ids, gate_probs, w_gate, w_up, w_down):
    vm = pl.BlockSpec(memory_space=pltpu.VMEM)
    hbm = pl.BlockSpec(memory_space=pltpu.HBM)
    dma = pltpu.SemaphoreType.DMA
    fin, grads = pl.pallas_call(
        kernel,
        out_shape=(
            jax.ShapeDtypeStruct((2, 8, 896), BF),
            jax.ShapeDtypeStruct((1024, 896), BF),
        ),
        in_specs=[vm] * 4 + [hbm] * 3,
        out_specs=(vm, hbm),
        scratch_shapes=[
            pltpu.VMEM((1024, 896), BF),
            pltpu.VMEM((4, 2, 16, 1024), BF),
            pltpu.VMEM((2, 8, 16, 896), BF),
            pltpu.VMEM((4, 2, 8, 16, 896), BF),
            pltpu.VMEM((4, 4, 32, 1024), BF),
            pltpu.VMEM((4, 4, 32, 1024), BF),
            pltpu.VMEM((4, 4, 32, 1024), BF),
            pltpu.VMEM((4, 2, 8, 16, 896), BF),
            pltpu.VMEM((4, 2, 8, 16, 896), BF),
            pltpu.VMEM((2, 8, 16, 896), BF),
            pltpu.VMEM((2, 8, 16, 896), BF),
            pltpu.VMEM((2, 32, 896), BF),
            pltpu.VMEM((2, 32, 896), BF),
            pltpu.VMEM((2, 4, 16, 512), F32),
            pltpu.VMEM((2, 2, 16, 256), BF),
            pltpu.VMEM((2, 3, 16, 512), BF),
            pltpu.VMEM((2, 2, 16, 512), BF),
            pltpu.VMEM((1024, 896), BF),
        ]
        + [dma((6,))] * 2
        + [dma((4,))] * 2
        + [dma((8,))] * 2
        + [dma((2, 8))] * 4
        + [dma((4, 4))] * 4
        + [dma((4, 2, 8))] * 2
        + [dma((2, 7))] * 2
        + [dma((2,))] * 2
        + [dma((2, 6))] * 2
        + [dma((3,)), dma],
        compiler_params=pltpu.CompilerParams(
            collective_id=0, has_side_effects=True, vmem_limit_bytes=60 << 20
        ),
        cost_estimate=pl.CostEstimate(
            flops=2600000000, bytes_accessed=4000000, transcendentals=40000
        ),
    )(
        tokens, out_grad, expert_ids.T, gate_probs.T,
        w_gate.transpose(0, 2, 1), w_up.transpose(0, 2, 1), w_down,
    )
    mixed, gtok, gg, gu, gd = pl.pallas_call(
        unstack,
        out_shape=(
            jax.ShapeDtypeStruct((8, 896), BF),
            jax.ShapeDtypeStruct((8, 896), BF),
            jax.ShapeDtypeStruct((1, 304, 896), BF),
            jax.ShapeDtypeStruct((1, 304, 896), BF),
            jax.ShapeDtypeStruct((1, 304, 896), BF),
        ),
        in_specs=[vm] * 2,
        out_specs=(hbm,) * 5,
        scratch_shapes=[dma((5,))],
        compiler_params=pltpu.CompilerParams(vmem_limit_bytes=60 << 20),
    )(fin, grads)
    return mixed, gtok, gg.transpose(0, 2, 1), gu.transpose(0, 2, 1), gd


def solution(mesh):
    wide = P(("dp", "expert"), "tp")
    rows = P(("dp", "expert"), None)
    up = P("expert", "tp", "dp")
    down = P("expert", "dp", "tp")
    return jax.shard_map(
        shards,
        mesh=mesh,
        in_specs=(wide, wide, rows, rows, up, up, down),
        out_specs=(wide, wide, up, up, down),
        check_vma=False,
    )
```
